32 devices in a mesh: seq: 8 (over y, x, core), tp: 4 (over z).
Axes of the slice: x: 2, y: 2, z: 4, core: 2. Of those that a mesh axis runs over, the one named last changes fastest.
Arguments:
- hidden: bfloat16 [2048, 4096], P('seq', 'tp'), may hold values from -6 to 6
- norm_gain: float32 [4096], replicated, may hold values from 0.25 to 1.75
- value_weight: bfloat16 [4096, 4096], P(None, 'tp'), may hold values from -0.09375 to 0.09375
- gate_weight: bfloat16 [4096, 4096], P(None, 'tp'), may hold values from -0.09375 to 0.09375
- value_taps: float32 [3, 4096], P(None, 'tp'), may hold values from -3 to 3
- gate_taps: float32 [3, 4096], P(None, 'tp'), may hold values from -3 to 3
- rates: float32 [16, 4096], P(None, 'tp'), may hold values from 2.4414063e-05 to 0.05, as said below
- residues: float32 [16, 4096], P(None, 'tp'), may hold values from -1.5 to 1.5
- out_weight: bfloat16 [4096, 4096], P('tp'), may hold values from -0.125 to 0.125
Outputs:
- mixed: bfloat16 [2048, 4096], P('seq', 'tp')
The draws below stay inside these ranges and needn't reach their ends.
Inputs may be any that keep to these rules, and one draw needn't show every extreme that they name: Decay rates are positive.
All inputs are finite; a program needn't handle non-finite values.
Results may differ from the reference program's by a relative error of at most 0.0076.
Values may be sent and summed in bfloat16 or wider, within the bound.
A program may use at most 256 MiB of HBM per device.

```python
import math
import jax
import jax.numpy as jnp
from jax import lax

D = 4096
MODES = 16
LENGTH = 2048


def draw_rates(key, part):
    lowest = 0.05 / LENGTH
    highest = 0.05
    unit = jax.random.uniform(key, (MODES, D), jnp.float32)
    return jnp.exp(jnp.log(lowest) + unit * (jnp.log(highest) - jnp.log(lowest)))


def with_spikes(drawn, rng, source, target, parts, factor):
    def block_of(axis_at):
        return (jnp.arange(drawn.shape[axis_at]) // (drawn.shape[axis_at] // parts)).reshape((-1,) + (1,) * (drawn.ndim - 1 - axis_at))

    first = jax.random.permutation(rng, parts)[block_of(target)]
    far = (block_of(target) + parts // 2) % parts
    return jnp.where((block_of(source) == first) | (block_of(source) == far), factor * drawn, drawn)


def block_levels(stream_key, shape, shards, smallest, largest):
    factor_of, own = 1.0, jax.random.fold_in(stream_key, 6)
    for axis_at, shards_of in shards:
        draws = jnp.exp(jax.random.uniform(jax.random.fold_in(own, axis_at), (shards_of,), jnp.float32, smallest / len(shards), largest / len(shards)))
        factor_of = factor_of * jnp.repeat(draws, shape[axis_at] // shards_of).reshape([-1 if axis == axis_at else 1 for axis in range(len(shape))])
    return factor_of


def normal_values(own_key, shape, spread, bound, shards=(), dtype=jnp.bfloat16):
    values = spread * jax.random.normal(own_key, shape, jnp.float32)
    if shards:
        values = values * block_levels(own_key, shape, shards, -0.22, 0.18)
    return jnp.clip(values, -bound, bound).astype(dtype)


def bell_draw_with(key, extent, scale, limit, split, heavy, held_as=jnp.bfloat16):
    values = scale * jax.random.normal(key, extent, jnp.float32)
    if split:
        values = values * block_levels(key, extent, split, -0.22, 0.18)
    return jnp.clip(with_spikes(values, jax.random.fold_in(key, 3), *heavy), -limit, limit).astype(held_as)


def setup_inputs(seed: int = 0) -> dict:
    keys = jax.random.split(jax.random.key(seed), 10)
    return {
        "hidden": normal_values(keys[0], (LENGTH, D), 1.0, 6.0, ((0, 8), (1, 4))),
        "norm_gain": jnp.clip(1.0 + 0.15 * jax.random.normal(keys[1], (D,), jnp.float32), 0.25, 1.75),
        "value_weight": normal_values(keys[2], (D, D), D ** -0.5, 0.09375, ((1, 4),)),
        "gate_weight": normal_values(keys[3], (D, D), D ** -0.5, 0.09375, ((1, 4),)),
        "value_taps": normal_values(keys[4], (3, D), 0.6, 3.0, ((1, 4),), jnp.float32),
        "gate_taps": normal_values(keys[5], (3, D), 0.6, 3.0, ((1, 4),), jnp.float32),
        "rates": draw_rates(jax.random.fold_in(keys[9], 71), 0),
        "residues": normal_values(keys[7], (MODES, D), MODES ** -0.5, 1.5, ((1, 4),), jnp.float32),
        "out_weight": bell_draw_with(keys[8], (D, D), D ** -0.5, 0.125, ((0, 4),), (0, 1, 4, 2.0)),
    }


eps = 1e-05

def normalize(whole, gain):
    values = whole.astype(jnp.float32)
    scale = lax.rsqrt(lax.optimization_barrier(jnp.mean(values * values, axis=1, keepdims=True)) + eps)
    return (values * scale * gain.astype(jnp.float32)[None, :]).astype(jnp.bfloat16)

def short_filter(signal, taps):
    padded = jnp.pad(signal.astype(jnp.float32), ((1, 1), (0, 0)))
    return taps[0][None, :] * padded[:-2] + taps[1][None, :] * padded[1:-1] + taps[2][None, :] * padded[2:]

def long_conv(signal, rates, residues):
    length = signal.shape[0]
    width = math.gcd(signal.shape[1], 128)
    count = signal.shape[1] // width
    strength = residues * jnp.sqrt(rates)
    lags = jnp.arange(2 * length)
    distance = jnp.minimum(lags, 2 * length - lags).astype(jnp.float32)
    keep = (lags != length).astype(jnp.float32)
    pieces = signal.reshape(length, count, width).transpose(1, 0, 2)
    rate_parts = rates.reshape(rates.shape[0], count, width).transpose(1, 0, 2)
    strength_parts = strength.reshape(rates.shape[0], count, width).transpose(1, 0, 2)

    def one_block(packed):
        piece, rate_part, strength_part = packed
        kernel = lax.optimization_barrier(jnp.sum(strength_part[None] * jnp.exp(-rate_part[None] * distance[:, None, None]), axis=1))
        kernel = kernel * keep[:, None]
        padded = jnp.pad(piece, ((0, length), (0, 0)))
        product = jnp.fft.rfft(padded, axis=0) * jnp.fft.rfft(kernel, axis=0)
        return jnp.fft.irfft(product, n=2 * length, axis=0)[:length]
    result = lax.map(one_block, (pieces, rate_parts, strength_parts))
    return result.transpose(1, 0, 2).reshape(length, signal.shape[1])

def reference(hidden, norm_gain, value_weight, gate_weight, value_taps, gate_taps, rates, residues, out_weight):

    def branch(source):
        normed = normalize(source, norm_gain)
        values = jnp.dot(normed, value_weight, preferred_element_type=jnp.float32).astype(jnp.bfloat16)
        gates = jnp.dot(normed, gate_weight, preferred_element_type=jnp.float32).astype(jnp.bfloat16)
        smooth_values = short_filter(values, value_taps)
        smooth_gates = short_filter(gates, gate_taps)
        conv = long_conv(smooth_values, rates, residues)
        return (smooth_gates * conv).astype(jnp.bfloat16)
    forward = branch(hidden)
    backward = branch(hidden[::-1, ::-1])
    total = jnp.dot(forward, out_weight, preferred_element_type=jnp.float32)
    total = total + jnp.dot(backward, out_weight, preferred_element_type=jnp.float32)[::-1, ::-1]
    return total.astype(jnp.bfloat16)
```

```python
import functools
import jax
import jax.numpy as jnp
from jax import lax
from jax.experimental import pallas as pl
from jax.experimental.pallas import tpu as pltpu
from jax.sharding import PartitionSpec as P

eps = 1e-05
f32 = jnp.float32
bf16 = jnp.bfloat16
LANES = 128
CHUNK = 16
HALF = CHUNK // 2
EDGE = 8
LIMIT = 56 * 1024 * 1024


def anti_identity(size):
    rows = lax.broadcasted_iota(jnp.int32, (size, size), 0)
    cols = lax.broadcasted_iota(jnp.int32, (size, size), 1)
    return (rows + cols == size - 1).astype(bf16)


def mirror(block, flip):
    size = flip.shape[0]
    count = block.shape[1] // size
    parts = [
        jnp.dot(block[:, (count - 1 - i) * size : (count - i) * size], flip, preferred_element_type=f32)
        for i in range(count)
    ]
    return jnp.concatenate(parts, axis=1) if count > 1 else parts[0]


def project_kernel(width, x_ref, far_ref, gain_ref, wv_ref, wg_ref, out_ref, both, acc, squares):
    step = pl.program_id(0)
    rows, depth = x_ref.shape[1], x_ref.shape[2]
    chans = wv_ref.shape[1]
    flip = anti_identity(min(256, depth))
    gain = gain_ref[...]
    values = x_ref[0].astype(f32)
    both[:rows] = (values * gain).astype(bf16)
    both[rows:] = (mirror(far_ref[0], flip) * gain).astype(bf16)
    part = jnp.sum(values * values, axis=1, keepdims=True)
    first = jnp.dot(both[...], wv_ref[...], preferred_element_type=f32)
    second = jnp.dot(both[...], wg_ref[...], preferred_element_type=f32)

    @pl.when(step == 0)
    def _():
        squares[...] = part
        acc[:, :chans] = first
        acc[:, chans:] = second

    @pl.when(step > 0)
    def _():
        squares[...] += part
        acc[:, :chans] += first
        acc[:, chans:] += second

    @pl.when(step == pl.num_programs(0) - 1)
    def _():
        scale = lax.rsqrt(squares[...] / width + eps)
        out_ref[0] = (acc[:rows] * scale).astype(bf16)
        out_ref[1] = (acc[rows:] * scale).astype(bf16)


def project(whole, gain, value_weight, gate_weight):
    owners, rows, chans = whole.shape
    width = owners * chans
    depth = min(512, chans)
    per = chans // depth
    steps = owners * per
    return pl.pallas_call(
        functools.partial(project_kernel, width),
        grid=(steps,),
        in_specs=[
            pl.BlockSpec((1, rows, depth), lambda i: (i // per, 0, i % per)),
            pl.BlockSpec((1, rows, depth), lambda i: ((steps - 1 - i) // per, 0, (steps - 1 - i) % per)),
            pl.BlockSpec((1, depth), lambda i: (0, i)),
            pl.BlockSpec((depth, chans), lambda i: (i, 0)),
            pl.BlockSpec((depth, chans), lambda i: (i, 0)),
        ],
        out_specs=pl.BlockSpec((2, rows, 2 * chans), lambda i: (0, 0, 0)),
        out_shape=jax.ShapeDtypeStruct((2, rows, 2 * chans), bf16),
        scratch_shapes=[
            pltpu.VMEM((2 * rows, depth), bf16),
            pltpu.VMEM((2 * rows, 2 * chans), f32),
            pltpu.VMEM((rows, 1), f32),
        ],
        compiler_params=pltpu.CompilerParams(vmem_limit_bytes=LIMIT),
        cost_estimate=pl.CostEstimate(
            flops=8 * rows * width * chans, bytes_accessed=4 * width * chans, transcendentals=0
        ),
        name="project",
    )(whole, whole, gain.reshape(1, width), value_weight, gate_weight)


def fill_tables(rates, cosh_ref, sinh_ref):
    for d in range(HALF):
        up = jnp.exp(rates * (d + 0.5))
        down = jnp.exp(rates * -(d + 0.5))
        cosh_ref[d] = 0.5 * (up + down)
        sinh_ref[d] = 0.5 * (up - down)


def smooth(wide, rows, taps, reverse):
    count = rows // CHUNK
    held = [wide[pl.ds(EDGE + s, count, stride=CHUNK), :] for s in range(-1, CHUNK + 1)]
    lead, mid, last = taps[0:1], taps[1:2], taps[2:3]
    if reverse:
        lead, last = last, lead
    return [lead * held[s] + mid * held[s + 1] + last * held[s + 2] for s in range(CHUNK)]


def pairs(signal):
    total = [signal[HALF + d] + signal[HALF - 1 - d] for d in range(HALF)]
    gap = [signal[HALF + d] - signal[HALF - 1 - d] for d in range(HALF)]
    return total, gap


def states_kernel(
    v_ref, g_ref, taps_ref, rates_ref, sent_ref, fore_ref, back_ref, wide, evens, odds, cosh_ref, sinh_ref
):
    rows = v_ref.shape[1]
    modes = rates_ref.shape[0]
    count = rows // CHUNK
    rates = rates_ref[...]
    taps = taps_ref[...]
    fill_tables(rates, cosh_ref, sinh_ref)
    centre = jnp.exp(rates * -(HALF - 0.5))
    leap = jnp.exp(rates * -float(CHUNK))
    totals = [[], []]
    zero = jnp.zeros((EDGE, LANES), f32)
    for strand in range(2):
        wide[:EDGE] = zero
        wide[EDGE + rows :] = zero
        wide[EDGE : EDGE + rows] = v_ref[strand].astype(f32)
        total, gap = pairs(smooth(wide, rows, taps, strand == 1))
        for m in range(modes):
            even = cosh_ref[0, m : m + 1] * total[0]
            odd = sinh_ref[0, m : m + 1] * gap[0]
            for d in range(1, HALF):
                even = even + cosh_ref[d, m : m + 1] * total[d]
                odd = odd + sinh_ref[d, m : m + 1] * gap[d]
            evens[m * count : (m + 1) * count] = even
            odds[m * count : (m + 1) * count] = odd
        state = jnp.zeros_like(rates)
        for n in range(count):
            fore_ref[strand, n] = state
            at = pl.ds(n, modes, stride=count)
            state = leap * state + centre * (evens[at, :] + odds[at, :])
        totals[0].append(state)
        state = jnp.zeros_like(rates)
        for n in reversed(range(count)):
            back_ref[strand, n] = state
            at = pl.ds(n, modes, stride=count)
            state = leap * state + centre * (evens[at, :] - odds[at, :])
        totals[1].append(state)
    edges = []
    for row in (0, rows - 1):
        for strand in range(2):
            for ref in (v_ref, g_ref):
                edges.append(ref[strand].astype(f32)[row : row + 1])
    edges.append(jnp.zeros((sent_ref.shape[0] - 4 * modes - 8, LANES), f32))
    sent_ref[...] = jnp.concatenate(totals[0] + totals[1] + edges, axis=0).astype(bf16)


def sent_rows(modes):
    return -(-(4 * modes + 8) // 16) * 16


def local_states(proj, value_taps, rates):
    _, rows, twice = proj.shape
    chans = twice // 2
    modes = rates.shape[0]
    count = rows // CHUNK
    tiles = chans // LANES
    sent = sent_rows(modes)
    states = jax.ShapeDtypeStruct((2, count, modes, chans), f32)
    state_spec = pl.BlockSpec((2, count, modes, LANES), lambda i: (0, 0, 0, i))
    return pl.pallas_call(
        states_kernel,
        grid=(tiles,),
        in_specs=[
            pl.BlockSpec((2, rows, LANES), lambda i: (0, 0, i)),
            pl.BlockSpec((2, rows, LANES), lambda i: (0, 0, i + tiles)),
            pl.BlockSpec((3, LANES), lambda i: (0, i)),
            pl.BlockSpec((modes, LANES), lambda i: (0, i)),
        ],
        out_specs=[pl.BlockSpec((sent, LANES), lambda i: (0, i)), state_spec, state_spec],
        out_shape=[jax.ShapeDtypeStruct((sent, chans), bf16), states, states],
        scratch_shapes=[
            pltpu.VMEM((rows + 2 * EDGE, LANES), f32),
            pltpu.VMEM((modes * count, LANES), f32),
            pltpu.VMEM((modes * count, LANES), f32),
            pltpu.VMEM((HALF, modes, LANES), f32),
            pltpu.VMEM((HALF, modes, LANES), f32),
        ],
        compiler_params=pltpu.CompilerParams(vmem_limit_bytes=LIMIT),
        name="local_states",
    )(proj, proj, value_taps, rates)


def gated_kernel(
    place_ref, v_ref, g_ref, vtaps_ref, gtaps_ref, rates_ref, res_ref, fore_ref, back_ref, all_ref,
    out_ref, wide, gate_wide, plus, minus, cosh_ref, sinh_ref, table, result,
):
    me = place_ref[0]
    devices = all_ref.shape[0]
    rows = v_ref.shape[1]
    modes = rates_ref.shape[0]
    count = rows // CHUNK
    rates = rates_ref[...]
    vtaps = vtaps_ref[...]
    gtaps = gtaps_ref[...]
    fill_tables(rates, cosh_ref, sinh_ref)
    strength = res_ref[...] * jnp.sqrt(rates)
    spread = strength * jnp.exp(rates * -(HALF + 0.5))
    behind = jnp.exp(rates)
    leap = jnp.exp(rates * -float(rows))
    across = jnp.exp(rates * -float(rows - 1))
    near = [
        0.5 * jnp.sum(strength * jnp.exp(rates * -float(k)), axis=0, keepdims=True)
        for k in range(CHUNK)
    ]
    for d in range(HALF):
        for e in range(HALF):
            at = d * HALF + e
            one, two = near[abs(d - e)], near[d + e + 1]
            table[at : at + 1] = one + two
            table[HALF * HALF + at : HALF * HALF + at + 1] = one - two

    def edge(source, which, strand, kind):
        at = 4 * modes + which * 4 + strand * 2 + kind
        return source[at : at + 1]

    gathered = [all_ref[src].astype(f32) for src in range(devices)]
    before = all_ref[jnp.maximum(me - 1, 0)].astype(f32) * (me > 0).astype(f32)
    after = all_ref[jnp.minimum(me + 1, devices - 1)].astype(f32) * (me < devices - 1).astype(f32)

    for strand in range(2):
        lead, last = (vtaps[0:1], vtaps[2:3]) if strand == 0 else (vtaps[2:3], vtaps[0:1])
        firsts = [
            lead * edge(gathered[src - 1], 1, strand, 0) if src else jnp.zeros((1, LANES), f32)
            for src in range(devices)
        ]
        lasts = [
            last * edge(gathered[src + 1], 0, strand, 0)
            if src < devices - 1
            else jnp.zeros((1, LANES), f32)
            for src in range(devices)
        ]
        fore = jnp.zeros_like(rates)
        for src in range(devices - 1):
            own = gathered[src][strand * modes : (strand + 1) * modes]
            own = own + across * firsts[src] + lasts[src]
            fore = jnp.where(src < me, fore * leap + own, fore)
        back = jnp.zeros_like(rates)
        for src in range(devices - 1, 0, -1):
            own = gathered[src][(2 + strand) * modes : (3 + strand) * modes]
            own = own + firsts[src] + across * lasts[src]
            back = jnp.where(src > me, back * leap + own, back)
        fore_on = fore + behind * (lead * edge(before, 1, strand, 0))
        back_on = back + behind * (last * edge(after, 0, strand, 0))
        for n in range(count):
            into = fore_ref[strand, n]
            into = into + (fore if n == 0 else jnp.exp(rates * -float(CHUNK * n)) * fore_on)
            outof = back_ref[strand, n]
            gap = count - 1 - n
            outof = outof + (back if gap == 0 else jnp.exp(rates * -float(CHUNK * gap)) * back_on)
            plus[n * modes : (n + 1) * modes] = spread * (into + outof)
            minus[n * modes : (n + 1) * modes] = spread * (into - outof)

        for buf, ref, kind in ((wide, v_ref, 0), (gate_wide, g_ref, 1)):
            buf[EDGE : EDGE + rows] = ref[strand].astype(f32)
            buf[EDGE - 1 : EDGE] = edge(before, 1, strand, kind)
            buf[EDGE + rows : EDGE + rows + 1] = edge(after, 0, strand, kind)
        total, gap = pairs(smooth(wide, rows, vtaps, strand == 1))
        even, odd = [], []
        for d in range(HALF):
            base = d * HALF
            one = table[base : base + 1] * total[0]
            two = table[HALF * HALF + base : HALF * HALF + base + 1] * gap[0]
            for e in range(1, HALF):
                at = base + e
                one = one + table[at : at + 1] * total[e]
                two = two + table[HALF * HALF + at : HALF * HALF + at + 1] * gap[e]
            even.append(one)
            odd.append(two)
        for m in range(modes):
            add = plus[pl.ds(m, count, stride=modes), :]
            sub = minus[pl.ds(m, count, stride=modes), :]
            for d in range(HALF):
                even[d] = even[d] + cosh_ref[d, m : m + 1] * add
                odd[d] = odd[d] - sinh_ref[d, m : m + 1] * sub
        gates = smooth(gate_wide, rows, gtaps, strand == 1)
        for d in range(HALF):
            one, two = HALF + d, HALF - 1 - d
            result[pl.ds(one, count, stride=CHUNK), :] = gates[one] * (even[d] + odd[d])
            result[pl.ds(two, count, stride=CHUNK), :] = gates[two] * (even[d] - odd[d])
        out_ref[strand] = result[...].astype(bf16)


def gated(place, proj, value_taps, gate_taps, rates, residues, fore, back, everyone):
    _, rows, twice = proj.shape
    chans = twice // 2
    modes = rates.shape[0]
    count = rows // CHUNK
    tiles = chans // LANES
    devices, sent, _ = everyone.shape
    state_spec = pl.BlockSpec((2, count, modes, LANES), lambda i: (0, 0, 0, i))
    tap_spec = pl.BlockSpec((3, LANES), lambda i: (0, i))
    mode_spec = pl.BlockSpec((modes, LANES), lambda i: (0, i))
    return pl.pallas_call(
        gated_kernel,
        grid=(tiles,),
        in_specs=[
            pl.BlockSpec(memory_space=pltpu.SMEM),
            pl.BlockSpec((2, rows, LANES), lambda i: (0, 0, i)),
            pl.BlockSpec((2, rows, LANES), lambda i: (0, 0, i + tiles)),
            tap_spec,
            tap_spec,
            mode_spec,
            mode_spec,
            state_spec,
            state_spec,
            pl.BlockSpec((devices, sent, LANES), lambda i: (0, 0, i)),
        ],
        out_specs=pl.BlockSpec((2, rows, LANES), lambda i: (0, 0, i)),
        out_shape=jax.ShapeDtypeStruct((2, rows, chans), bf16),
        scratch_shapes=[
            pltpu.VMEM((rows + 2 * EDGE, LANES), f32),
            pltpu.VMEM((rows + 2 * EDGE, LANES), f32),
            pltpu.VMEM((modes * count, LANES), f32),
            pltpu.VMEM((modes * count, LANES), f32),
            pltpu.VMEM((HALF, modes, LANES), f32),
            pltpu.VMEM((HALF, modes, LANES), f32),
            pltpu.VMEM((2 * HALF * HALF, LANES), f32),
            pltpu.VMEM((rows, LANES), f32),
        ],
        compiler_params=pltpu.CompilerParams(vmem_limit_bytes=LIMIT),
        name="gated",
    )(place, proj, proj, value_taps, gate_taps, rates, residues, fore, back, everyone)


def output_kernel(z_ref, low_ref, high_ref, out_ref):
    step = pl.program_id(0)
    _, rows, chans = z_ref.shape
    size = low_ref.shape[1]
    per = out_ref.shape[2] // size
    tiles = 2 * pl.num_programs(0)
    flip = anti_identity(min(256, size))

    def turned(product):
        high = product.astype(bf16)
        low = (product - high.astype(f32)).astype(bf16)
        return mirror(high, flip) + mirror(low, flip)

    z = z_ref[...].reshape(2 * rows, chans)
    low = jnp.dot(z, low_ref[...], preferred_element_type=f32)
    high = jnp.dot(z, high_ref[...], preferred_element_type=f32)
    other = tiles - 1 - step
    for tile, own, far in ((step, low, high), (other, high, low)):
        cols = pl.ds(pl.multiple_of(lax.rem(tile, per) * size, size), size)
        out_ref[tile // per, :, cols] = (own[:rows] + turned(far[rows:])).astype(bf16)


def output(z, out_weight, parts):
    _, rows, chans = z.shape
    width = out_weight.shape[1]
    each = width // parts
    size = min(512, each)
    tiles = width // size
    return pl.pallas_call(
        output_kernel,
        grid=(tiles // 2,),
        in_specs=[
            pl.BlockSpec((2, rows, chans), lambda i: (0, 0, 0)),
            pl.BlockSpec((chans, size), lambda i: (0, i)),
            pl.BlockSpec((chans, size), lambda i: (0, tiles - 1 - i)),
        ],
        out_specs=pl.BlockSpec((parts, rows, each), lambda i: (0, 0, 0)),
        out_shape=jax.ShapeDtypeStruct((parts, rows, each), bf16),
        compiler_params=pltpu.CompilerParams(vmem_limit_bytes=LIMIT),
        name="output",
    )(z, out_weight, out_weight)


def body(
    hidden, norm_gain, value_weight, gate_weight, value_taps, gate_taps, rates, residues, out_weight
):
    whole = lax.all_gather(hidden, "tp", axis=0)
    proj = project(whole, norm_gain, value_weight, gate_weight)
    sent, fore, back = local_states(proj, value_taps, rates)
    everyone = lax.all_gather(sent, "seq", axis=0)
    place = lax.axis_index("seq").astype(jnp.int32).reshape(1)
    z = gated(place, proj, value_taps, gate_taps, rates, residues, fore, back, everyone)
    term = output(z, out_weight, lax.axis_size("tp"))
    return lax.psum_scatter(term, "tp", scatter_dimension=0, tiled=False)


def solution(mesh):
    in_specs = (
        P("seq", "tp"),
        P(),
        P(None, "tp"),
        P(None, "tp"),
        P(None, "tp"),
        P(None, "tp"),
        P(None, "tp"),
        P(None, "tp"),
        P("tp", None),
    )
    out_specs = P("seq", "tp")
    return jax.shard_map(body, mesh=mesh, in_specs=in_specs, out_specs=out_specs, check_vma=False)
```

```python
import functools
import jax
import jax.numpy as jnp
from jax import lax
from jax.experimental import pallas as pl
from jax.experimental.pallas import tpu as pltpu
from jax.sharding import PartitionSpec as P

eps = 1e-05
f32 = jnp.float32
bf16 = jnp.bfloat16
LANES = 128
CHUNK = 16
HALF = CHUNK // 2
EDGE = 8
LIMIT = 56 * 1024 * 1024


def anti_identity(size):
    rows = lax.broadcasted_iota(jnp.int32, (size, size), 0)
    cols = lax.broadcasted_iota(jnp.int32, (size, size), 1)
    return (rows + cols == size - 1).astype(bf16)


def mirror(block, flip):
    size = flip.shape[0]
    count = block.shape[1] // size
    parts = [
        jnp.dot(block[:, (count - 1 - i) * size : (count - i) * size], flip, preferred_element_type=f32)
        for i in range(count)
    ]
    return jnp.concatenate(parts, axis=1) if count > 1 else parts[0]


def project_kernel(x_ref, gain_ref, wv_ref, wg_ref, *rest):
    v_ref, g_ref, both = rest[-3:]
    owners, rows, chans = x_ref.shape

    @pl.when(pl.program_id(0) == 0)
    def _():
        flip = anti_identity(min(256, chans))
        squares = jnp.zeros((rows, 1), f32)
        for owner in range(owners):
            values = x_ref[owner].astype(f32)
            squares = squares + jnp.sum(values * values, axis=1, keepdims=True)
        scale = lax.rsqrt(squares / (owners * chans) + eps)
        for owner in range(owners):
            cols = slice(owner * chans, (owner + 1) * chans)
            gain = gain_ref[:, cols]
            both[:rows, cols] = (x_ref[owner].astype(f32) * scale * gain).astype(bf16)
            far = mirror(x_ref[owners - 1 - owner], flip)
            both[rows:, cols] = (far * scale * gain).astype(bf16)

    for weight_ref, out_ref in ((wv_ref, v_ref), (wg_ref, g_ref)):
        product = jnp.dot(both[...], weight_ref[...], preferred_element_type=f32).astype(bf16)
        out_ref[0] = product[:rows]
        out_ref[1] = product[rows:]


def project(whole, part, parts, gain, value_weight, gate_weight, earlier):
    owners, rows, chans = whole.shape
    width = owners * chans
    size = min(256, chans)
    weight_spec = pl.BlockSpec((width, size), lambda i: (0, i))
    out_spec = pl.BlockSpec((2, rows, size), lambda i: (0, part, i))
    out_shape = jax.ShapeDtypeStruct((2, rows * parts, chans), bf16)
    return pl.pallas_call(
        project_kernel,
        grid=(chans // size,),
        in_specs=[
            pl.BlockSpec((owners, rows, chans), lambda i: (0, 0, 0)),
            pl.BlockSpec((1, width), lambda i: (0, 0)),
            weight_spec,
            weight_spec,
        ]
        + [pl.BlockSpec(memory_space=pl.ANY)] * len(earlier),
        out_specs=[out_spec, out_spec],
        out_shape=[out_shape, out_shape],
        input_output_aliases={4 + i: i for i in range(len(earlier))},
        scratch_shapes=[pltpu.VMEM((2 * rows, width), bf16)],
        compiler_params=pltpu.CompilerParams(vmem_limit_bytes=LIMIT),
        cost_estimate=pl.CostEstimate(
            flops=8 * rows * width * chans, bytes_accessed=4 * width * chans, transcendentals=0
        ),
        name="project",
    )(whole, gain.reshape(1, width), value_weight, gate_weight, *earlier)


def fill_tables(rates, cosh_ref, sinh_ref):
    for d in range(HALF):
        up = jnp.exp(rates * (d + 0.5))
        down = jnp.exp(rates * -(d + 0.5))
        cosh_ref[d] = 0.5 * (up + down)
        sinh_ref[d] = 0.5 * (up - down)


def smooth(wide, rows, taps, reverse):
    count = rows // CHUNK
    held = [wide[pl.ds(EDGE + s, count, stride=CHUNK), :] for s in range(-1, CHUNK + 1)]
    lead, mid, last = taps[0:1], taps[1:2], taps[2:3]
    if reverse:
        lead, last = last, lead
    return [lead * held[s] + mid * held[s + 1] + last * held[s + 2] for s in range(CHUNK)]


def pairs(signal):
    total = [signal[HALF + d] + signal[HALF - 1 - d] for d in range(HALF)]
    gap = [signal[HALF + d] - signal[HALF - 1 - d] for d in range(HALF)]
    return total, gap


def states_kernel(
    v_ref, g_ref, taps_ref, rates_ref, sent_ref, fore_ref, back_ref, wide, evens, odds, cosh_ref, sinh_ref
):
    rows = v_ref.shape[1]
    modes = rates_ref.shape[0]
    count = rows // CHUNK
    rates = rates_ref[...]
    taps = taps_ref[...]
    fill_tables(rates, cosh_ref, sinh_ref)
    centre = jnp.exp(rates * -(HALF - 0.5))
    leap = jnp.exp(rates * -float(CHUNK))
    totals = [[], []]
    zero = jnp.zeros((EDGE, LANES), f32)
    for strand in range(2):
        wide[:EDGE] = zero
        wide[EDGE + rows :] = zero
        wide[EDGE : EDGE + rows] = v_ref[strand].astype(f32)
        total, gap = pairs(smooth(wide, rows, taps, strand == 1))
        for m in range(modes):
            even = cosh_ref[0, m : m + 1] * total[0]
            odd = sinh_ref[0, m : m + 1] * gap[0]
            for d in range(1, HALF):
                even = even + cosh_ref[d, m : m + 1] * total[d]
                odd = odd + sinh_ref[d, m : m + 1] * gap[d]
            evens[m * count : (m + 1) * count] = even
            odds[m * count : (m + 1) * count] = odd
        state = jnp.zeros_like(rates)
        for n in range(count):
            fore_ref[strand, n] = state
            at = pl.ds(n, modes, stride=count)
            state = leap * state + centre * (evens[at, :] + odds[at, :])
        totals[0].append(state)
        state = jnp.zeros_like(rates)
        for n in reversed(range(count)):
            back_ref[strand, n] = state
            at = pl.ds(n, modes, stride=count)
            state = leap * state + centre * (evens[at, :] - odds[at, :])
        totals[1].append(state)
    edges = []
    for row in (0, rows - 1):
        for strand in range(2):
            for ref in (v_ref, g_ref):
                edges.append(ref[strand].astype(f32)[row : row + 1])
    edges.append(jnp.zeros((sent_ref.shape[0] - 4 * modes - 8, LANES), f32))
    sent_ref[...] = jnp.concatenate(totals[0] + totals[1] + edges, axis=0).astype(bf16)


def sent_rows(modes):
    return -(-(4 * modes + 8) // 16) * 16


def local_states(values, gates, value_taps, rates):
    _, rows, chans = values.shape
    modes = rates.shape[0]
    count = rows // CHUNK
    tiles = chans // LANES
    sent = sent_rows(modes)
    states = jax.ShapeDtypeStruct((2, count, modes, chans), f32)
    state_spec = pl.BlockSpec((2, count, modes, LANES), lambda i: (0, 0, 0, i))
    return pl.pallas_call(
        states_kernel,
        grid=(tiles,),
        in_specs=[
            pl.BlockSpec((2, rows, LANES), lambda i: (0, 0, i)),
            pl.BlockSpec((2, rows, LANES), lambda i: (0, 0, i)),
            pl.BlockSpec((3, LANES), lambda i: (0, i)),
            pl.BlockSpec((modes, LANES), lambda i: (0, i)),
        ],
        out_specs=[pl.BlockSpec((sent, LANES), lambda i: (0, i)), state_spec, state_spec],
        out_shape=[jax.ShapeDtypeStruct((sent, chans), bf16), states, states],
        scratch_shapes=[
            pltpu.VMEM((rows + 2 * EDGE, LANES), f32),
            pltpu.VMEM((modes * count, LANES), f32),
            pltpu.VMEM((modes * count, LANES), f32),
            pltpu.VMEM((HALF, modes, LANES), f32),
            pltpu.VMEM((HALF, modes, LANES), f32),
        ],
        compiler_params=pltpu.CompilerParams(vmem_limit_bytes=LIMIT),
        name="local_states",
    )(values, gates, value_taps, rates)


def gated_kernel(
    place_ref, v_ref, g_ref, vtaps_ref, gtaps_ref, rates_ref, res_ref, fore_ref, back_ref, all_ref,
    out_ref, wide, gate_wide, plus, minus, cosh_ref, sinh_ref, table, result,
):
    me = place_ref[0]
    devices = all_ref.shape[0]
    rows = v_ref.shape[1]
    modes = rates_ref.shape[0]
    count = rows // CHUNK
    rates = rates_ref[...]
    vtaps = vtaps_ref[...]
    gtaps = gtaps_ref[...]
    fill_tables(rates, cosh_ref, sinh_ref)
    strength = res_ref[...] * jnp.sqrt(rates)
    spread = strength * jnp.exp(rates * -(HALF + 0.5))
    behind = jnp.exp(rates)
    leap = jnp.exp(rates * -float(rows))
    across = jnp.exp(rates * -float(rows - 1))
    near = [
        0.5 * jnp.sum(strength * jnp.exp(rates * -float(k)), axis=0, keepdims=True)
        for k in range(CHUNK)
    ]
    for d in range(HALF):
        for e in range(HALF):
            at = d * HALF + e
            one, two = near[abs(d - e)], near[d + e + 1]
            table[at : at + 1] = one + two
            table[HALF * HALF + at : HALF * HALF + at + 1] = one - two

    def edge(source, which, strand, kind):
        at = 4 * modes + which * 4 + strand * 2 + kind
        return source[at : at + 1]

    gathered = [all_ref[src].astype(f32) for src in range(devices)]
    before = all_ref[jnp.maximum(me - 1, 0)].astype(f32) * (me > 0).astype(f32)
    after = all_ref[jnp.minimum(me + 1, devices - 1)].astype(f32) * (me < devices - 1).astype(f32)

    for strand in range(2):
        lead, last = (vtaps[0:1], vtaps[2:3]) if strand == 0 else (vtaps[2:3], vtaps[0:1])
        firsts = [
            lead * edge(gathered[src - 1], 1, strand, 0) if src else jnp.zeros((1, LANES), f32)
            for src in range(devices)
        ]
        lasts = [
            last * edge(gathered[src + 1], 0, strand, 0)
            if src < devices - 1
            else jnp.zeros((1, LANES), f32)
            for src in range(devices)
        ]
        fore = jnp.zeros_like(rates)
        for src in range(devices - 1):
            own = gathered[src][strand * modes : (strand + 1) * modes]
            own = own + across * firsts[src] + lasts[src]
            fore = jnp.where(src < me, fore * leap + own, fore)
        back = jnp.zeros_like(rates)
        for src in range(devices - 1, 0, -1):
            own = gathered[src][(2 + strand) * modes : (3 + strand) * modes]
            own = own + firsts[src] + across * lasts[src]
            back = jnp.where(src > me, back * leap + own, back)
        fore_on = fore + behind * (lead * edge(before, 1, strand, 0))
        back_on = back + behind * (last * edge(after, 0, strand, 0))
        for n in range(count):
            into = fore_ref[strand, n]
            into = into + (fore if n == 0 else jnp.exp(rates * -float(CHUNK * n)) * fore_on)
            outof = back_ref[strand, n]
            gap = count - 1 - n
            outof = outof + (back if gap == 0 else jnp.exp(rates * -float(CHUNK * gap)) * back_on)
            plus[n * modes : (n + 1) * modes] = spread * (into + outof)
            minus[n * modes : (n + 1) * modes] = spread * (into - outof)

        for buf, ref, kind in ((wide, v_ref, 0), (gate_wide, g_ref, 1)):
            buf[EDGE : EDGE + rows] = ref[strand].astype(f32)
            buf[EDGE - 1 : EDGE] = edge(before, 1, strand, kind)
            buf[EDGE + rows : EDGE + rows + 1] = edge(after, 0, strand, kind)
        total, gap = pairs(smooth(wide, rows, vtaps, strand == 1))
        even, odd = [], []
        for d in range(HALF):
            base = d * HALF
            one = table[base : base + 1] * total[0]
            two = table[HALF * HALF + base : HALF * HALF + base + 1] * gap[0]
            for e in range(1, HALF):
                at = base + e
                one = one + table[at : at + 1] * total[e]
                two = two + table[HALF * HALF + at : HALF * HALF + at + 1] * gap[e]
            even.append(one)
            odd.append(two)
        for m in range(modes):
            add = plus[pl.ds(m, count, stride=modes), :]
            sub = minus[pl.ds(m, count, stride=modes), :]
            for d in range(HALF):
                even[d] = even[d] + cosh_ref[d, m : m + 1] * add
                odd[d] = odd[d] - sinh_ref[d, m : m + 1] * sub
        gates = smooth(gate_wide, rows, gtaps, strand == 1)
        for d in range(HALF):
            one, two = HALF + d, HALF - 1 - d
            result[pl.ds(one, count, stride=CHUNK), :] = gates[one] * (even[d] + odd[d])
            result[pl.ds(two, count, stride=CHUNK), :] = gates[two] * (even[d] - odd[d])
        out_ref[strand] = result[...].astype(bf16)


def gated(place, values, gates, value_taps, gate_taps, rates, residues, fore, back, everyone):
    _, rows, chans = values.shape
    modes = rates.shape[0]
    count = rows // CHUNK
    tiles = chans // LANES
    devices, sent, _ = everyone.shape
    state_spec = pl.BlockSpec((2, count, modes, LANES), lambda i: (0, 0, 0, i))
    tap_spec = pl.BlockSpec((3, LANES), lambda i: (0, i))
    mode_spec = pl.BlockSpec((modes, LANES), lambda i: (0, i))
    return pl.pallas_call(
        gated_kernel,
        grid=(tiles,),
        in_specs=[
            pl.BlockSpec(memory_space=pltpu.SMEM),
            pl.BlockSpec((2, rows, LANES), lambda i: (0, 0, i)),
            pl.BlockSpec((2, rows, LANES), lambda i: (0, 0, i)),
            tap_spec,
            tap_spec,
            mode_spec,
            mode_spec,
            state_spec,
            state_spec,
            pl.BlockSpec((devices, sent, LANES), lambda i: (0, 0, i)),
        ],
        out_specs=pl.BlockSpec((2, rows, LANES), lambda i: (0, 0, i)),
        out_shape=jax.ShapeDtypeStruct((2, rows, chans), bf16),
        scratch_shapes=[
            pltpu.VMEM((rows + 2 * EDGE, LANES), f32),
            pltpu.VMEM((rows + 2 * EDGE, LANES), f32),
            pltpu.VMEM((modes * count, LANES), f32),
            pltpu.VMEM((modes * count, LANES), f32),
            pltpu.VMEM((HALF, modes, LANES), f32),
            pltpu.VMEM((HALF, modes, LANES), f32),
            pltpu.VMEM((2 * HALF * HALF, LANES), f32),
            pltpu.VMEM((rows, LANES), f32),
        ],
        compiler_params=pltpu.CompilerParams(vmem_limit_bytes=LIMIT),
        name="gated",
    )(place, values, gates, value_taps, gate_taps, rates, residues, fore, back, everyone)


def output_kernel(z_ref, low_ref, high_ref, out_ref):
    step = pl.program_id(0)
    _, rows, chans = z_ref.shape
    size = low_ref.shape[1]
    per = out_ref.shape[2] // size
    tiles = 2 * pl.num_programs(0)
    flip = anti_identity(min(256, size))

    def turned(product):
        high = product.astype(bf16)
        low = (product - high.astype(f32)).astype(bf16)
        return mirror(high, flip) + mirror(low, flip)

    z = z_ref[...].reshape(2 * rows, chans)
    low = jnp.dot(z, low_ref[...], preferred_element_type=f32)
    high = jnp.dot(z, high_ref[...], preferred_element_type=f32)
    other = tiles - 1 - step
    for tile, own, far in ((step, low, high), (other, high, low)):
        cols = pl.ds(pl.multiple_of(lax.rem(tile, per) * size, size), size)
        out_ref[tile // per, :, cols] = (own[:rows] + turned(far[rows:])).astype(bf16)


def output(z, out_weight, parts):
    _, rows, chans = z.shape
    width = out_weight.shape[1]
    each = width // parts
    size = min(512, each)
    tiles = width // size
    return pl.pallas_call(
        output_kernel,
        grid=(tiles // 2,),
        in_specs=[
            pl.BlockSpec((2, rows, chans), lambda i: (0, 0, 0)),
            pl.BlockSpec((chans, size), lambda i: (0, i)),
            pl.BlockSpec((chans, size), lambda i: (0, tiles - 1 - i)),
        ],
        out_specs=pl.BlockSpec((parts, rows, each), lambda i: (0, 0, 0)),
        out_shape=jax.ShapeDtypeStruct((parts, rows, each), bf16),
        compiler_params=pltpu.CompilerParams(vmem_limit_bytes=LIMIT),
        name="output",
    )(z, out_weight, out_weight)


def body(
    hidden, norm_gain, value_weight, gate_weight, value_taps, gate_taps, rates, residues, out_weight
):
    parts = 2
    rows = hidden.shape[0] // parts
    wholes = [
        lax.all_gather(hidden[part * rows : (part + 1) * rows], "tp", axis=0) for part in range(parts)
    ]
    proj = ()
    for part, whole in enumerate(wholes):
        proj = project(whole, part, parts, norm_gain, value_weight, gate_weight, proj)
    sent, fore, back = local_states(*proj, value_taps, rates)
    everyone = lax.all_gather(sent, "seq", axis=0)
    place = lax.axis_index("seq").astype(jnp.int32).reshape(1)
    z = gated(place, *proj, value_taps, gate_taps, rates, residues, fore, back, everyone)
    term = output(z, out_weight, lax.axis_size("tp"))
    return lax.psum_scatter(term, "tp", scatter_dimension=0, tiled=False)


def solution(mesh):
    in_specs = (
        P("seq", "tp"),
        P(),
        P(None, "tp"),
        P(None, "tp"),
        P(None, "tp"),
        P(None, "tp"),
        P(None, "tp"),
        P(None, "tp"),
        P("tp", None),
    )
    out_specs = P("seq", "tp")
    return jax.shard_map(body, mesh=mesh, in_specs=in_specs, out_specs=out_specs, check_vma=False)
```

```python
import functools
import jax
import jax.numpy as jnp
from jax import lax
from jax.experimental import pallas as pl
from jax.experimental.pallas import tpu as pltpu
from jax.sharding import PartitionSpec as P

eps = 1e-05
f32 = jnp.float32
bf16 = jnp.bfloat16
LANES = 128
CHUNK = 16
HALF = CHUNK // 2
EDGE = 8
LIMIT = 56 * 1024 * 1024


def anti_identity(size):
    rows = lax.broadcasted_iota(jnp.int32, (size, size), 0)
    cols = lax.broadcasted_iota(jnp.int32, (size, size), 1)
    return (rows + cols == size - 1).astype(bf16)


def mirror(block, flip):
    size = flip.shape[0]
    count = block.shape[1] // size
    parts = [
        jnp.dot(block[:, (count - 1 - i) * size : (count - i) * size], flip, preferred_element_type=f32)
        for i in range(count)
    ]
    return jnp.concatenate(parts, axis=1) if count > 1 else parts[0]


MESH = pl.DeviceIdType.MESH


def line_kernel(axis, count, x_ref, out_ref, to_right, to_left, landed, own_sem):
    me = lax.axis_index(axis)
    has_left, has_right = me > 0, me < count - 1
    left, right = jnp.maximum(me - 1, 0), jnp.minimum(me + 1, count - 1)
    barrier = pltpu.get_barrier_semaphore()
    for hop in range(1, count):
        other = lax.rem(me + hop, count)
        pl.semaphore_signal(barrier, inc=1, device_id={axis: other}, device_id_type=MESH)
    pl.semaphore_wait(barrier, count - 1)

    def move(step, block, rightward):
        sems, target = (to_right, right) if rightward else (to_left, left)
        return pltpu.make_async_remote_copy(
            src_ref=x_ref if step == 0 else out_ref.at[block],
            dst_ref=out_ref.at[block],
            send_sem=sems.at[step],
            recv_sem=landed.at[block],
            device_id={axis: target},
            device_id_type=MESH,
        )

    own = pltpu.make_async_copy(x_ref, out_ref.at[me], own_sem)
    for step in range(count):
        for rightward in (True, False):
            block = me - step if rightward else me + step
            exists = block >= 0 if rightward else block < count
            onward = has_right if rightward else has_left

            if step > 0:

                @pl.when(exists)
                def _():
                    move(step, block, rightward).wait_recv()

            if step < count - 1:

                @pl.when(jnp.logical_and(exists, onward))
                def _():
                    move(step, block, rightward).start()

        if step == 0:
            own.start()
    for step in range(count - 1):
        for rightward in (True, False):
            block = me - step if rightward else me + step
            exists = block >= 0 if rightward else block < count
            onward = has_right if rightward else has_left

            @pl.when(jnp.logical_and(exists, onward))
            def _():
                move(step, block, rightward).wait_send()

    own.wait()


def direct_kernel(axis, count, x_ref, out_ref, sent, landed, own_sem):
    me = lax.axis_index(axis)
    barrier = pltpu.get_barrier_semaphore()
    others = [lax.rem(me + hop, count) for hop in range(1, count)]
    for other in others:
        pl.semaphore_signal(barrier, inc=1, device_id={axis: other}, device_id_type=MESH)
    pl.semaphore_wait(barrier, count - 1)

    def move(hop, block):
        return pltpu.make_async_remote_copy(
            src_ref=x_ref,
            dst_ref=out_ref.at[block],
            send_sem=sent.at[hop],
            recv_sem=landed.at[block],
            device_id={axis: others[hop]},
            device_id_type=MESH,
        )

    own = pltpu.make_async_copy(x_ref, out_ref.at[me], own_sem)
    for hop in range(count - 1):
        move(hop, me).start()
    own.start()
    for hop in range(count - 1):
        move(hop, others[hop]).wait_recv()
    for hop in range(count - 1):
        move(hop, me).wait_send()
    own.wait()


def gather(x, axis, kernel, number):
    count = lax.axis_size(axis)
    dma = pltpu.SemaphoreType.DMA
    sends = [dma((count,))] * (2 if kernel is line_kernel else 1)
    return pl.pallas_call(
        functools.partial(kernel, axis, count),
        in_specs=[pl.BlockSpec(memory_space=pl.ANY)],
        out_specs=pl.BlockSpec(memory_space=pl.ANY),
        out_shape=jax.ShapeDtypeStruct((count,) + x.shape, x.dtype),
        scratch_shapes=sends + [dma((count,)), dma(())],
        compiler_params=pltpu.CompilerParams(
            collective_id=number, has_side_effects=True, vmem_limit_bytes=LIMIT
        ),
        name="gather_" + axis,
    )(x)


def project_kernel(x_ref, gain_ref, wv_ref, wg_ref, *rest):
    v_ref, g_ref, both = rest[-3:]
    owners, rows, chans = x_ref.shape

    @pl.when(pl.program_id(0) == 0)
    def _():
        flip = anti_identity(min(256, chans))
        squares = jnp.zeros((rows, 1), f32)
        for owner in range(owners):
            values = x_ref[owner].astype(f32)
            squares = squares + jnp.sum(values * values, axis=1, keepdims=True)
        scale = lax.rsqrt(squares / (owners * chans) + eps)
        for owner in range(owners):
            cols = slice(owner * chans, (owner + 1) * chans)
            gain = gain_ref[:, cols]
            both[:rows, cols] = (x_ref[owner].astype(f32) * scale * gain).astype(bf16)
            far = mirror(x_ref[owners - 1 - owner], flip)
            both[rows:, cols] = (far * scale * gain).astype(bf16)

    for weight_ref, out_ref in ((wv_ref, v_ref), (wg_ref, g_ref)):
        product = jnp.dot(both[...], weight_ref[...], preferred_element_type=f32).astype(bf16)
        out_ref[0] = product[:rows]
        out_ref[1] = product[rows:]


def project(whole, part, parts, gain, value_weight, gate_weight, earlier):
    owners, rows, chans = whole.shape
    width = owners * chans
    size = min(256, chans)
    weight_spec = pl.BlockSpec((width, size), lambda i: (0, i))
    out_spec = pl.BlockSpec((2, rows, size), lambda i: (0, part, i))
    out_shape = jax.ShapeDtypeStruct((2, rows * parts, chans), bf16)
    return pl.pallas_call(
        project_kernel,
        grid=(chans // size,),
        in_specs=[
            pl.BlockSpec((owners, rows, chans), lambda i: (0, 0, 0)),
            pl.BlockSpec((1, width), lambda i: (0, 0)),
            weight_spec,
            weight_spec,
        ]
        + [pl.BlockSpec(memory_space=pl.ANY)] * len(earlier),
        out_specs=[out_spec, out_spec],
        out_shape=[out_shape, out_shape],
        input_output_aliases={4 + i: i for i in range(len(earlier))},
        scratch_shapes=[pltpu.VMEM((2 * rows, width), bf16)],
        compiler_params=pltpu.CompilerParams(vmem_limit_bytes=LIMIT),
        cost_estimate=pl.CostEstimate(
            flops=8 * rows * width * chans, bytes_accessed=4 * width * chans, transcendentals=0
        ),
        name="project",
    )(whole, gain.reshape(1, width), value_weight, gate_weight, *earlier)


def fill_tables(rates, cosh_ref, sinh_ref):
    for d in range(HALF):
        up = jnp.exp(rates * (d + 0.5))
        down = jnp.exp(rates * -(d + 0.5))
        cosh_ref[d] = 0.5 * (up + down)
        sinh_ref[d] = 0.5 * (up - down)


def smooth(wide, rows, taps, reverse):
    count = rows // CHUNK
    held = [wide[pl.ds(EDGE + s, count, stride=CHUNK), :] for s in range(-1, CHUNK + 1)]
    lead, mid, last = taps[0:1], taps[1:2], taps[2:3]
    if reverse:
        lead, last = last, lead
    return [lead * held[s] + mid * held[s + 1] + last * held[s + 2] for s in range(CHUNK)]


def pairs(signal):
    total = [signal[HALF + d] + signal[HALF - 1 - d] for d in range(HALF)]
    gap = [signal[HALF + d] - signal[HALF - 1 - d] for d in range(HALF)]
    return total, gap


def states_kernel(
    v_ref, g_ref, taps_ref, rates_ref, sent_ref, fore_ref, back_ref, wide, evens, odds, cosh_ref, sinh_ref
):
    rows = v_ref.shape[1]
    modes = rates_ref.shape[0]
    count = rows // CHUNK
    rates = rates_ref[...]
    taps = taps_ref[...]
    fill_tables(rates, cosh_ref, sinh_ref)
    centre = jnp.exp(rates * -(HALF - 0.5))
    leap = jnp.exp(rates * -float(CHUNK))
    totals = [[], []]
    zero = jnp.zeros((EDGE, LANES), f32)
    for strand in range(2):
        wide[:EDGE] = zero
        wide[EDGE + rows :] = zero
        wide[EDGE : EDGE + rows] = v_ref[strand].astype(f32)
        total, gap = pairs(smooth(wide, rows, taps, strand == 1))
        for m in range(modes):
            even = cosh_ref[0, m : m + 1] * total[0]
            odd = sinh_ref[0, m : m + 1] * gap[0]
            for d in range(1, HALF):
                even = even + cosh_ref[d, m : m + 1] * total[d]
                odd = odd + sinh_ref[d, m : m + 1] * gap[d]
            evens[m * count : (m + 1) * count] = even
            odds[m * count : (m + 1) * count] = odd
        state = jnp.zeros_like(rates)
        for n in range(count):
            fore_ref[strand, n] = state
            at = pl.ds(n, modes, stride=count)
            state = leap * state + centre * (evens[at, :] + odds[at, :])
        totals[0].append(state)
        state = jnp.zeros_like(rates)
        for n in reversed(range(count)):
            back_ref[strand, n] = state
            at = pl.ds(n, modes, stride=count)
            state = leap * state + centre * (evens[at, :] - odds[at, :])
        totals[1].append(state)
    edges = []
    for row in (0, rows - 1):
        for strand in range(2):
            for ref in (v_ref, g_ref):
                edges.append(ref[strand].astype(f32)[row : row + 1])
    edges.append(jnp.zeros((sent_ref.shape[0] - 4 * modes - 8, LANES), f32))
    sent_ref[...] = jnp.concatenate(totals[0] + totals[1] + edges, axis=0).astype(bf16)


def sent_rows(modes):
    return -(-(4 * modes + 8) // 16) * 16


def local_states(values, gates, value_taps, rates):
    _, rows, chans = values.shape
    modes = rates.shape[0]
    count = rows // CHUNK
    tiles = chans // LANES
    sent = sent_rows(modes)
    states = jax.ShapeDtypeStruct((2, count, modes, chans), f32)
    state_spec = pl.BlockSpec((2, count, modes, LANES), lambda i: (0, 0, 0, i))
    return pl.pallas_call(
        states_kernel,
        grid=(tiles,),
        in_specs=[
            pl.BlockSpec((2, rows, LANES), lambda i: (0, 0, i)),
            pl.BlockSpec((2, rows, LANES), lambda i: (0, 0, i)),
            pl.BlockSpec((3, LANES), lambda i: (0, i)),
            pl.BlockSpec((modes, LANES), lambda i: (0, i)),
        ],
        out_specs=[pl.BlockSpec((sent, LANES), lambda i: (0, i)), state_spec, state_spec],
        out_shape=[jax.ShapeDtypeStruct((sent, chans), bf16), states, states],
        scratch_shapes=[
            pltpu.VMEM((rows + 2 * EDGE, LANES), f32),
            pltpu.VMEM((modes * count, LANES), f32),
            pltpu.VMEM((modes * count, LANES), f32),
            pltpu.VMEM((HALF, modes, LANES), f32),
            pltpu.VMEM((HALF, modes, LANES), f32),
        ],
        compiler_params=pltpu.CompilerParams(vmem_limit_bytes=LIMIT),
        name="local_states",
    )(values, gates, value_taps, rates)


def gated_kernel(
    place_ref, v_ref, g_ref, vtaps_ref, gtaps_ref, rates_ref, res_ref, fore_ref, back_ref, all_ref,
    out_ref, wide, gate_wide, plus, minus, cosh_ref, sinh_ref, table, result,
):
    me = place_ref[0]
    devices = all_ref.shape[0]
    rows = v_ref.shape[1]
    modes = rates_ref.shape[0]
    count = rows // CHUNK
    rates = rates_ref[...]
    vtaps = vtaps_ref[...]
    gtaps = gtaps_ref[...]
    fill_tables(rates, cosh_ref, sinh_ref)
    strength = res_ref[...] * jnp.sqrt(rates)
    spread = strength * jnp.exp(rates * -(HALF + 0.5))
    behind = jnp.exp(rates)
    leap = jnp.exp(rates * -float(rows))
    across = jnp.exp(rates * -float(rows - 1))
    near = [
        0.5 * jnp.sum(strength * jnp.exp(rates * -float(k)), axis=0, keepdims=True)
        for k in range(CHUNK)
    ]
    for d in range(HALF):
        for e in range(HALF):
            at = d * HALF + e
            one, two = near[abs(d - e)], near[d + e + 1]
            table[at : at + 1] = one + two
            table[HALF * HALF + at : HALF * HALF + at + 1] = one - two

    def edge(source, which, strand, kind):
        at = 4 * modes + which * 4 + strand * 2 + kind
        return source[at : at + 1]

    gathered = [all_ref[src].astype(f32) for src in range(devices)]
    before = all_ref[jnp.maximum(me - 1, 0)].astype(f32) * (me > 0).astype(f32)
    after = all_ref[jnp.minimum(me + 1, devices - 1)].astype(f32) * (me < devices - 1).astype(f32)

    for strand in range(2):
        lead, last = (vtaps[0:1], vtaps[2:3]) if strand == 0 else (vtaps[2:3], vtaps[0:1])
        firsts = [
            lead * edge(gathered[src - 1], 1, strand, 0) if src else jnp.zeros((1, LANES), f32)
            for src in range(devices)
        ]
        lasts = [
            last * edge(gathered[src + 1], 0, strand, 0)
            if src < devices - 1
            else jnp.zeros((1, LANES), f32)
            for src in range(devices)
        ]
        fore = jnp.zeros_like(rates)
        for src in range(devices - 1):
            own = gathered[src][strand * modes : (strand + 1) * modes]
            own = own + across * firsts[src] + lasts[src]
            fore = jnp.where(src < me, fore * leap + own, fore)
        back = jnp.zeros_like(rates)
        for src in range(devices - 1, 0, -1):
            own = gathered[src][(2 + strand) * modes : (3 + strand) * modes]
            own = own + firsts[src] + across * lasts[src]
            back = jnp.where(src > me, back * leap + own, back)
        fore_on = fore + behind * (lead * edge(before, 1, strand, 0))
        back_on = back + behind * (last * edge(after, 0, strand, 0))
        for n in range(count):
            into = fore_ref[strand, n]
            into = into + (fore if n == 0 else jnp.exp(rates * -float(CHUNK * n)) * fore_on)
            outof = back_ref[strand, n]
            gap = count - 1 - n
            outof = outof + (back if gap == 0 else jnp.exp(rates * -float(CHUNK * gap)) * back_on)
            plus[n * modes : (n + 1) * modes] = spread * (into + outof)
            minus[n * modes : (n + 1) * modes] = spread * (into - outof)

        for buf, ref, kind in ((wide, v_ref, 0), (gate_wide, g_ref, 1)):
            buf[EDGE : EDGE + rows] = ref[strand].astype(f32)
            buf[EDGE - 1 : EDGE] = edge(before, 1, strand, kind)
            buf[EDGE + rows : EDGE + rows + 1] = edge(after, 0, strand, kind)
        total, gap = pairs(smooth(wide, rows, vtaps, strand == 1))
        even, odd = [], []
        for d in range(HALF):
            base = d * HALF
            one = table[base : base + 1] * total[0]
            two = table[HALF * HALF + base : HALF * HALF + base + 1] * gap[0]
            for e in range(1, HALF):
                at = base + e
                one = one + table[at : at + 1] * total[e]
                two = two + table[HALF * HALF + at : HALF * HALF + at + 1] * gap[e]
            even.append(one)
            odd.append(two)
        for m in range(modes):
            add = plus[pl.ds(m, count, stride=modes), :]
            sub = minus[pl.ds(m, count, stride=modes), :]
            for d in range(HALF):
                even[d] = even[d] + cosh_ref[d, m : m + 1] * add
                odd[d] = odd[d] - sinh_ref[d, m : m + 1] * sub
        gates = smooth(gate_wide, rows, gtaps, strand == 1)
        for d in range(HALF):
            one, two = HALF + d, HALF - 1 - d
            result[pl.ds(one, count, stride=CHUNK), :] = gates[one] * (even[d] + odd[d])
            result[pl.ds(two, count, stride=CHUNK), :] = gates[two] * (even[d] - odd[d])
        out_ref[strand] = result[...].astype(bf16)


def gated(place, values, gates, value_taps, gate_taps, rates, residues, fore, back, everyone):
    _, rows, chans = values.shape
    modes = rates.shape[0]
    count = rows // CHUNK
    tiles = chans // LANES
    devices, sent, _ = everyone.shape
    state_spec = pl.BlockSpec((2, count, modes, LANES), lambda i: (0, 0, 0, i))
    tap_spec = pl.BlockSpec((3, LANES), lambda i: (0, i))
    mode_spec = pl.BlockSpec((modes, LANES), lambda i: (0, i))
    return pl.pallas_call(
        gated_kernel,
        grid=(tiles,),
        in_specs=[
            pl.BlockSpec(memory_space=pltpu.SMEM),
            pl.BlockSpec((2, rows, LANES), lambda i: (0, 0, i)),
            pl.BlockSpec((2, rows, LANES), lambda i: (0, 0, i)),
            tap_spec,
            tap_spec,
            mode_spec,
            mode_spec,
            state_spec,
            state_spec,
            pl.BlockSpec((devices, sent, LANES), lambda i: (0, 0, i)),
        ],
        out_specs=pl.BlockSpec((2, rows, LANES), lambda i: (0, 0, i)),
        out_shape=jax.ShapeDtypeStruct((2, rows, chans), bf16),
        scratch_shapes=[
            pltpu.VMEM((rows + 2 * EDGE, LANES), f32),
            pltpu.VMEM((rows + 2 * EDGE, LANES), f32),
            pltpu.VMEM((modes * count, LANES), f32),
            pltpu.VMEM((modes * count, LANES), f32),
            pltpu.VMEM((HALF, modes, LANES), f32),
            pltpu.VMEM((HALF, modes, LANES), f32),
            pltpu.VMEM((2 * HALF * HALF, LANES), f32),
            pltpu.VMEM((rows, LANES), f32),
        ],
        compiler_params=pltpu.CompilerParams(vmem_limit_bytes=LIMIT),
        name="gated",
    )(place, values, gates, value_taps, gate_taps, rates, residues, fore, back, everyone)


def output_kernel(z_ref, low_ref, high_ref, out_ref):
    step = pl.program_id(0)
    _, rows, chans = z_ref.shape
    size = low_ref.shape[1]
    per = out_ref.shape[2] // size
    tiles = 2 * pl.num_programs(0)
    flip = anti_identity(min(256, size))

    def turned(product):
        high = product.astype(bf16)
        low = (product - high.astype(f32)).astype(bf16)
        return mirror(high, flip) + mirror(low, flip)

    z = z_ref[...].reshape(2 * rows, chans)
    low = jnp.dot(z, low_ref[...], preferred_element_type=f32)
    high = jnp.dot(z, high_ref[...], preferred_element_type=f32)
    other = tiles - 1 - step
    for tile, own, far in ((step, low, high), (other, high, low)):
        cols = pl.ds(pl.multiple_of(lax.rem(tile, per) * size, size), size)
        out_ref[tile // per, :, cols] = (own[:rows] + turned(far[rows:])).astype(bf16)


def output(z, out_weight, parts):
    _, rows, chans = z.shape
    width = out_weight.shape[1]
    each = width // parts
    size = min(512, each)
    tiles = width // size
    return pl.pallas_call(
        output_kernel,
        grid=(tiles // 2,),
        in_specs=[
            pl.BlockSpec((2, rows, chans), lambda i: (0, 0, 0)),
            pl.BlockSpec((chans, size), lambda i: (0, i)),
            pl.BlockSpec((chans, size), lambda i: (0, tiles - 1 - i)),
        ],
        out_specs=pl.BlockSpec((parts, rows, each), lambda i: (0, 0, 0)),
        out_shape=jax.ShapeDtypeStruct((parts, rows, each), bf16),
        compiler_params=pltpu.CompilerParams(vmem_limit_bytes=LIMIT),
        name="output",
    )(z, out_weight, out_weight)


def body(
    hidden, norm_gain, value_weight, gate_weight, value_taps, gate_taps, rates, residues, out_weight
):
    parts = 1
    rows = hidden.shape[0] // parts
    wholes = [
        gather(hidden[part * rows : (part + 1) * rows], "tp", line_kernel, part) for part in range(parts)
    ]
    proj = ()
    for part, whole in enumerate(wholes):
        proj = project(whole, part, parts, norm_gain, value_weight, gate_weight, proj)
    sent, fore, back = local_states(*proj, value_taps, rates)
    everyone = gather(sent, "seq", direct_kernel, parts)
    place = lax.axis_index("seq").astype(jnp.int32).reshape(1)
    z = gated(place, *proj, value_taps, gate_taps, rates, residues, fore, back, everyone)
    term = output(z, out_weight, lax.axis_size("tp"))
    return lax.psum_scatter(term, "tp", scatter_dimension=0, tiled=False)


def solution(mesh):
    in_specs = (
        P("seq", "tp"),
        P(),
        P(None, "tp"),
        P(None, "tp"),
        P(None, "tp"),
        P(None, "tp"),
        P(None, "tp"),
        P(None, "tp"),
        P("tp", None),
    )
    out_specs = P("seq", "tp")
    return jax.shard_map(body, mesh=mesh, in_specs=in_specs, out_specs=out_specs, check_vma=False)
```

```python
import functools
import jax
import jax.numpy as jnp
from jax import lax
from jax.experimental import pallas as pl
from jax.experimental.pallas import tpu as pltpu
from jax.sharding import PartitionSpec as P

eps = 1e-05
f32 = jnp.float32
bf16 = jnp.bfloat16
LANES = 128
CHUNK = 16
HALF = CHUNK // 2
EDGE = 8
LIMIT = 56 * 1024 * 1024


def anti_identity(size):
    rows = lax.broadcasted_iota(jnp.int32, (size, size), 0)
    cols = lax.broadcasted_iota(jnp.int32, (size, size), 1)
    return (rows + cols == size - 1).astype(bf16)


def mirror(block, flip):
    size = flip.shape[0]
    count = block.shape[1] // size
    parts = [
        jnp.dot(block[:, (count - 1 - i) * size : (count - i) * size], flip, preferred_element_type=f32)
        for i in range(count)
    ]
    return jnp.concatenate(parts, axis=1) if count > 1 else parts[0]


MESH = pl.DeviceIdType.MESH


def line_kernel(axis, count, x_ref, out_ref, to_right, to_left, landed, own_sem):
    me = lax.axis_index(axis)
    has_left, has_right = me > 0, me < count - 1
    left, right = jnp.maximum(me - 1, 0), jnp.minimum(me + 1, count - 1)
    barrier = pltpu.get_barrier_semaphore()
    for hop in range(1, count):
        other = lax.rem(me + hop, count)
        pl.semaphore_signal(barrier, inc=1, device_id={axis: other}, device_id_type=MESH)
    pl.semaphore_wait(barrier, count - 1)

    def move(step, block, rightward):
        sems, target = (to_right, right) if rightward else (to_left, left)
        return pltpu.make_async_remote_copy(
            src_ref=x_ref if step == 0 else out_ref.at[block],
            dst_ref=out_ref.at[block],
            send_sem=sems.at[step],
            recv_sem=landed.at[block],
            device_id={axis: target},
            device_id_type=MESH,
        )

    own = pltpu.make_async_copy(x_ref, out_ref.at[me], own_sem)
    for step in range(count):
        for rightward in (True, False):
            block = me - step if rightward else me + step
            exists = block >= 0 if rightward else block < count
            onward = has_right if rightward else has_left

            if step > 0:

                @pl.when(exists)
                def _():
                    move(step, block, rightward).wait_recv()

            if step < count - 1:

                @pl.when(jnp.logical_and(exists, onward))
                def _():
                    move(step, block, rightward).start()

        if step == 0:
            own.start()
    for step in range(count - 1):
        for rightward in (True, False):
            block = me - step if rightward else me + step
            exists = block >= 0 if rightward else block < count
            onward = has_right if rightward else has_left

            @pl.when(jnp.logical_and(exists, onward))
            def _():
                move(step, block, rightward).wait_send()

    own.wait()


def direct_kernel(axis, count, x_ref, out_ref, sent, landed, own_sem):
    me = lax.axis_index(axis)
    barrier = pltpu.get_barrier_semaphore()
    others = [lax.rem(me + hop, count) for hop in range(1, count)]
    for other in others:
        pl.semaphore_signal(barrier, inc=1, device_id={axis: other}, device_id_type=MESH)
    pl.semaphore_wait(barrier, count - 1)

    def move(hop, block):
        return pltpu.make_async_remote_copy(
            src_ref=x_ref,
            dst_ref=out_ref.at[block],
            send_sem=sent.at[hop],
            recv_sem=landed.at[block],
            device_id={axis: others[hop]},
            device_id_type=MESH,
        )

    own = pltpu.make_async_copy(x_ref, out_ref.at[me], own_sem)
    for hop in range(count - 1):
        move(hop, me).start()
    own.start()
    for hop in range(count - 1):
        move(hop, others[hop]).wait_recv()
    for hop in range(count - 1):
        move(hop, me).wait_send()
    own.wait()


def gather(x, axis, kernel, number):
    count = lax.axis_size(axis)
    dma = pltpu.SemaphoreType.DMA
    sends = [dma((count,))] * (2 if kernel is line_kernel else 1)
    return pl.pallas_call(
        functools.partial(kernel, axis, count),
        in_specs=[pl.BlockSpec(memory_space=pl.ANY)],
        out_specs=pl.BlockSpec(memory_space=pl.ANY),
        out_shape=jax.ShapeDtypeStruct((count,) + x.shape, x.dtype),
        scratch_shapes=sends + [dma((count,)), dma(())],
        compiler_params=pltpu.CompilerParams(
            collective_id=number, has_side_effects=True, vmem_limit_bytes=LIMIT
        ),
        name="gather_" + axis,
    )(x)


def scatter_kernel(axis, count, term_ref, out_ref, from_left, from_right, to_right, to_left, in_left, in_right):
    me = lax.axis_index(axis)
    left, right = jnp.maximum(me - 1, 0), jnp.minimum(me + 1, count - 1)
    barrier = pltpu.get_barrier_semaphore()
    for hop in range(1, count):
        other = lax.rem(me + hop, count)
        pl.semaphore_signal(barrier, inc=1, device_id={axis: other}, device_id_type=MESH)
    pl.semaphore_wait(barrier, count - 1)

    def move(block, rightward):
        slots, sends, lands, target = (
            (from_left, to_right, in_left, right) if rightward else (from_right, to_left, in_right, left)
        )
        return pltpu.make_async_remote_copy(
            src_ref=slots.at[block],
            dst_ref=slots.at[block],
            send_sem=sends.at[block],
            recv_sem=lands.at[block],
            device_id={axis: target},
            device_id_type=MESH,
        )

    def ways(k):
        return ((count - 1 - k, True), (k, False))

    for k in range(count):
        for block, rightward in ways(k):
            slots = from_left if rightward else from_right
            begins = me == 0 if rightward else me == count - 1
            passes = me < block if rightward else me > block
            takes = me <= block if rightward else me >= block

            @pl.when(jnp.logical_and(takes, jnp.logical_not(begins)))
            def _():
                move(block, rightward).wait_recv()

            @pl.when(jnp.logical_and(passes, begins))
            def _():
                slots[block] = term_ref[block]

            @pl.when(jnp.logical_and(passes, jnp.logical_not(begins)))
            def _():
                slots[block] = (slots[block].astype(f32) + term_ref[block].astype(f32)).astype(bf16)

            @pl.when(passes)
            def _():
                move(block, rightward).start()

    for block in range(count):

        @pl.when(me == block)
        def _():
            total = term_ref[block].astype(f32)
            if block > 0:
                total = total + from_left[block].astype(f32)
            if block < count - 1:
                total = total + from_right[block].astype(f32)
            out_ref[...] = total.astype(bf16)

    for k in range(count):
        for block, rightward in ways(k):

            @pl.when(me < block if rightward else me > block)
            def _():
                move(block, rightward).wait_send()


def scatter_sum(term, axis, number):
    count, rows, each = term.shape
    sems = pltpu.SemaphoreType.DMA((count,))
    return pl.pallas_call(
        functools.partial(scatter_kernel, axis, count),
        in_specs=[pl.BlockSpec(memory_space=pltpu.VMEM)],
        out_specs=pl.BlockSpec(memory_space=pltpu.VMEM),
        out_shape=jax.ShapeDtypeStruct((rows, each), term.dtype),
        scratch_shapes=[pltpu.VMEM(term.shape, term.dtype)] * 2 + [sems] * 4,
        compiler_params=pltpu.CompilerParams(
            collective_id=number, has_side_effects=True, vmem_limit_bytes=LIMIT
        ),
        name="scatter_sum",
    )(term)


def project_kernel(x_ref, gain_ref, wv_ref, wg_ref, *rest):
    v_ref, g_ref, both = rest[-3:]
    owners, rows, chans = x_ref.shape

    @pl.when(pl.program_id(0) == 0)
    def _():
        flip = anti_identity(min(256, chans))
        squares = jnp.zeros((rows, 1), f32)
        for owner in range(owners):
            values = x_ref[owner].astype(f32)
            squares = squares + jnp.sum(values * values, axis=1, keepdims=True)
        scale = lax.rsqrt(squares / (owners * chans) + eps)
        for owner in range(owners):
            cols = slice(owner * chans, (owner + 1) * chans)
            gain = gain_ref[:, cols]
            both[:rows, cols] = (x_ref[owner].astype(f32) * scale * gain).astype(bf16)
            far = mirror(x_ref[owners - 1 - owner], flip)
            both[rows:, cols] = (far * scale * gain).astype(bf16)

    for weight_ref, out_ref in ((wv_ref, v_ref), (wg_ref, g_ref)):
        product = jnp.dot(both[...], weight_ref[...], preferred_element_type=f32).astype(bf16)
        out_ref[0] = product[:rows]
        out_ref[1] = product[rows:]


def project(whole, part, parts, gain, value_weight, gate_weight, earlier):
    owners, rows, chans = whole.shape
    width = owners * chans
    size = min(256, chans)
    weight_spec = pl.BlockSpec((width, size), lambda i: (0, i))
    out_spec = pl.BlockSpec((2, rows, size), lambda i: (0, part, i))
    out_shape = jax.ShapeDtypeStruct((2, rows * parts, chans), bf16)
    return pl.pallas_call(
        project_kernel,
        grid=(chans // size,),
        in_specs=[
            pl.BlockSpec((owners, rows, chans), lambda i: (0, 0, 0)),
            pl.BlockSpec((1, width), lambda i: (0, 0)),
            weight_spec,
            weight_spec,
        ]
        + [pl.BlockSpec(memory_space=pl.ANY)] * len(earlier),
        out_specs=[out_spec, out_spec],
        out_shape=[out_shape, out_shape],
        input_output_aliases={4 + i: i for i in range(len(earlier))},
        scratch_shapes=[pltpu.VMEM((2 * rows, width), bf16)],
        compiler_params=pltpu.CompilerParams(vmem_limit_bytes=LIMIT),
        cost_estimate=pl.CostEstimate(
            flops=8 * rows * width * chans, bytes_accessed=4 * width * chans, transcendentals=0
        ),
        name="project",
    )(whole, gain.reshape(1, width), value_weight, gate_weight, *earlier)


def fill_tables(rates, cosh_ref, sinh_ref):
    for d in range(HALF):
        up = jnp.exp(rates * (d + 0.5))
        down = jnp.exp(rates * -(d + 0.5))
        cosh_ref[d] = 0.5 * (up + down)
        sinh_ref[d] = 0.5 * (up - down)


def smooth(wide, rows, taps, reverse):
    count = rows // CHUNK
    held = [wide[pl.ds(EDGE + s, count, stride=CHUNK), :] for s in range(-1, CHUNK + 1)]
    lead, mid, last = taps[0:1], taps[1:2], taps[2:3]
    if reverse:
        lead, last = last, lead
    return [lead * held[s] + mid * held[s + 1] + last * held[s + 2] for s in range(CHUNK)]


def pairs(signal):
    total = [signal[HALF + d] + signal[HALF - 1 - d] for d in range(HALF)]
    gap = [signal[HALF + d] - signal[HALF - 1 - d] for d in range(HALF)]
    return total, gap


def states_kernel(
    v_ref, g_ref, taps_ref, rates_ref, sent_ref, fore_ref, back_ref, wide, evens, odds, cosh_ref, sinh_ref
):
    rows = v_ref.shape[1]
    modes = rates_ref.shape[0]
    count = rows // CHUNK
    rates = rates_ref[...]
    taps = taps_ref[...]
    fill_tables(rates, cosh_ref, sinh_ref)
    centre = jnp.exp(rates * -(HALF - 0.5))
    leap = jnp.exp(rates * -float(CHUNK))
    totals = [[], []]
    zero = jnp.zeros((EDGE, LANES), f32)
    for strand in range(2):
        wide[:EDGE] = zero
        wide[EDGE + rows :] = zero
        wide[EDGE : EDGE + rows] = v_ref[strand].astype(f32)
        total, gap = pairs(smooth(wide, rows, taps, strand == 1))
        for m in range(modes):
            even = cosh_ref[0, m : m + 1] * total[0]
            odd = sinh_ref[0, m : m + 1] * gap[0]
            for d in range(1, HALF):
                even = even + cosh_ref[d, m : m + 1] * total[d]
                odd = odd + sinh_ref[d, m : m + 1] * gap[d]
            evens[m * count : (m + 1) * count] = even
            odds[m * count : (m + 1) * count] = odd
        state = jnp.zeros_like(rates)
        for n in range(count):
            fore_ref[strand, n] = state
            at = pl.ds(n, modes, stride=count)
            state = leap * state + centre * (evens[at, :] + odds[at, :])
        totals[0].append(state)
        state = jnp.zeros_like(rates)
        for n in reversed(range(count)):
            back_ref[strand, n] = state
            at = pl.ds(n, modes, stride=count)
            state = leap * state + centre * (evens[at, :] - odds[at, :])
        totals[1].append(state)
    edges = []
    for row in (0, rows - 1):
        for strand in range(2):
            for ref in (v_ref, g_ref):
                edges.append(ref[strand].astype(f32)[row : row + 1])
    edges.append(jnp.zeros((sent_ref.shape[0] - 4 * modes - 8, LANES), f32))
    sent_ref[...] = jnp.concatenate(totals[0] + totals[1] + edges, axis=0).astype(bf16)


def sent_rows(modes):
    return -(-(4 * modes + 8) // 16) * 16


def local_states(values, gates, value_taps, rates):
    _, rows, chans = values.shape
    modes = rates.shape[0]
    count = rows // CHUNK
    tiles = chans // LANES
    sent = sent_rows(modes)
    states = jax.ShapeDtypeStruct((2, count, modes, chans), f32)
    state_spec = pl.BlockSpec((2, count, modes, LANES), lambda i: (0, 0, 0, i))
    return pl.pallas_call(
        states_kernel,
        grid=(tiles,),
        in_specs=[
            pl.BlockSpec((2, rows, LANES), lambda i: (0, 0, i)),
            pl.BlockSpec((2, rows, LANES), lambda i: (0, 0, i)),
            pl.BlockSpec((3, LANES), lambda i: (0, i)),
            pl.BlockSpec((modes, LANES), lambda i: (0, i)),
        ],
        out_specs=[pl.BlockSpec((sent, LANES), lambda i: (0, i)), state_spec, state_spec],
        out_shape=[jax.ShapeDtypeStruct((sent, chans), bf16), states, states],
        scratch_shapes=[
            pltpu.VMEM((rows + 2 * EDGE, LANES), f32),
            pltpu.VMEM((modes * count, LANES), f32),
            pltpu.VMEM((modes * count, LANES), f32),
            pltpu.VMEM((HALF, modes, LANES), f32),
            pltpu.VMEM((HALF, modes, LANES), f32),
        ],
        compiler_params=pltpu.CompilerParams(vmem_limit_bytes=LIMIT),
        name="local_states",
    )(values, gates, value_taps, rates)


def gated_kernel(
    place_ref, v_ref, g_ref, vtaps_ref, gtaps_ref, rates_ref, res_ref, fore_ref, back_ref, all_ref,
    out_ref, wide, gate_wide, plus, minus, cosh_ref, sinh_ref, table, result,
):
    me = place_ref[0]
    devices = all_ref.shape[0]
    rows = v_ref.shape[1]
    modes = rates_ref.shape[0]
    count = rows // CHUNK
    rates = rates_ref[...]
    vtaps = vtaps_ref[...]
    gtaps = gtaps_ref[...]
    fill_tables(rates, cosh_ref, sinh_ref)
    strength = res_ref[...] * jnp.sqrt(rates)
    spread = strength * jnp.exp(rates * -(HALF + 0.5))
    behind = jnp.exp(rates)
    leap = jnp.exp(rates * -float(rows))
    across = jnp.exp(rates * -float(rows - 1))
    near = [
        0.5 * jnp.sum(strength * jnp.exp(rates * -float(k)), axis=0, keepdims=True)
        for k in range(CHUNK)
    ]
    for d in range(HALF):
        for e in range(HALF):
            at = d * HALF + e
            one, two = near[abs(d - e)], near[d + e + 1]
            table[at : at + 1] = one + two
            table[HALF * HALF + at : HALF * HALF + at + 1] = one - two

    def edge(source, which, strand, kind):
        at = 4 * modes + which * 4 + strand * 2 + kind
        return source[at : at + 1]

    gathered = [all_ref[src].astype(f32) for src in range(devices)]
    before = all_ref[jnp.maximum(me - 1, 0)].astype(f32) * (me > 0).astype(f32)
    after = all_ref[jnp.minimum(me + 1, devices - 1)].astype(f32) * (me < devices - 1).astype(f32)

    for strand in range(2):
        lead, last = (vtaps[0:1], vtaps[2:3]) if strand == 0 else (vtaps[2:3], vtaps[0:1])
        firsts = [
            lead * edge(gathered[src - 1], 1, strand, 0) if src else jnp.zeros((1, LANES), f32)
            for src in range(devices)
        ]
        lasts = [
            last * edge(gathered[src + 1], 0, strand, 0)
            if src < devices - 1
            else jnp.zeros((1, LANES), f32)
            for src in range(devices)
        ]
        fore = jnp.zeros_like(rates)
        for src in range(devices - 1):
            own = gathered[src][strand * modes : (strand + 1) * modes]
            own = own + across * firsts[src] + lasts[src]
            fore = jnp.where(src < me, fore * leap + own, fore)
        back = jnp.zeros_like(rates)
        for src in range(devices - 1, 0, -1):
            own = gathered[src][(2 + strand) * modes : (3 + strand) * modes]
            own = own + firsts[src] + across * lasts[src]
            back = jnp.where(src > me, back * leap + own, back)
        fore_on = fore + behind * (lead * edge(before, 1, strand, 0))
        back_on = back + behind * (last * edge(after, 0, strand, 0))
        for n in range(count):
            into = fore_ref[strand, n]
            into = into + (fore if n == 0 else jnp.exp(rates * -float(CHUNK * n)) * fore_on)
            outof = back_ref[strand, n]
            gap = count - 1 - n
            outof = outof + (back if gap == 0 else jnp.exp(rates * -float(CHUNK * gap)) * back_on)
            plus[n * modes : (n + 1) * modes] = spread * (into + outof)
            minus[n * modes : (n + 1) * modes] = spread * (into - outof)

        for buf, ref, kind in ((wide, v_ref, 0), (gate_wide, g_ref, 1)):
            buf[EDGE : EDGE + rows] = ref[strand].astype(f32)
            buf[EDGE - 1 : EDGE] = edge(before, 1, strand, kind)
            buf[EDGE + rows : EDGE + rows + 1] = edge(after, 0, strand, kind)
        total, gap = pairs(smooth(wide, rows, vtaps, strand == 1))
        even, odd = [], []
        for d in range(HALF):
            base = d * HALF
            one = table[base : base + 1] * total[0]
            two = table[HALF * HALF + base : HALF * HALF + base + 1] * gap[0]
            for e in range(1, HALF):
                at = base + e
                one = one + table[at : at + 1] * total[e]
                two = two + table[HALF * HALF + at : HALF * HALF + at + 1] * gap[e]
            even.append(one)
            odd.append(two)
        for m in range(modes):
            add = plus[pl.ds(m, count, stride=modes), :]
            sub = minus[pl.ds(m, count, stride=modes), :]
            for d in range(HALF):
                even[d] = even[d] + cosh_ref[d, m : m + 1] * add
                odd[d] = odd[d] - sinh_ref[d, m : m + 1] * sub
        gates = smooth(gate_wide, rows, gtaps, strand == 1)
        for d in range(HALF):
            one, two = HALF + d, HALF - 1 - d
            result[pl.ds(one, count, stride=CHUNK), :] = gates[one] * (even[d] + odd[d])
            result[pl.ds(two, count, stride=CHUNK), :] = gates[two] * (even[d] - odd[d])
        out_ref[strand] = result[...].astype(bf16)


def gated(place, values, gates, value_taps, gate_taps, rates, residues, fore, back, everyone):
    _, rows, chans = values.shape
    modes = rates.shape[0]
    count = rows // CHUNK
    tiles = chans // LANES
    devices, sent, _ = everyone.shape
    state_spec = pl.BlockSpec((2, count, modes, LANES), lambda i: (0, 0, 0, i))
    tap_spec = pl.BlockSpec((3, LANES), lambda i: (0, i))
    mode_spec = pl.BlockSpec((modes, LANES), lambda i: (0, i))
    return pl.pallas_call(
        gated_kernel,
        grid=(tiles,),
        in_specs=[
            pl.BlockSpec(memory_space=pltpu.SMEM),
            pl.BlockSpec((2, rows, LANES), lambda i: (0, 0, i)),
            pl.BlockSpec((2, rows, LANES), lambda i: (0, 0, i)),
            tap_spec,
            tap_spec,
            mode_spec,
            mode_spec,
            state_spec,
            state_spec,
            pl.BlockSpec((devices, sent, LANES), lambda i: (0, 0, i)),
        ],
        out_specs=pl.BlockSpec((2, rows, LANES), lambda i: (0, 0, i)),
        out_shape=jax.ShapeDtypeStruct((2, rows, chans), bf16),
        scratch_shapes=[
            pltpu.VMEM((rows + 2 * EDGE, LANES), f32),
            pltpu.VMEM((rows + 2 * EDGE, LANES), f32),
            pltpu.VMEM((modes * count, LANES), f32),
            pltpu.VMEM((modes * count, LANES), f32),
            pltpu.VMEM((HALF, modes, LANES), f32),
            pltpu.VMEM((HALF, modes, LANES), f32),
            pltpu.VMEM((2 * HALF * HALF, LANES), f32),
            pltpu.VMEM((rows, LANES), f32),
        ],
        compiler_params=pltpu.CompilerParams(vmem_limit_bytes=LIMIT),
        name="gated",
    )(place, values, gates, value_taps, gate_taps, rates, residues, fore, back, everyone)


def output_kernel(z_ref, low_ref, high_ref, out_ref):
    step = pl.program_id(0)
    _, rows, chans = z_ref.shape
    size = low_ref.shape[1]
    per = out_ref.shape[2] // size
    tiles = 2 * pl.num_programs(0)
    flip = anti_identity(min(256, size))

    def turned(product):
        high = product.astype(bf16)
        low = (product - high.astype(f32)).astype(bf16)
        return mirror(high, flip) + mirror(low, flip)

    z = z_ref[...].reshape(2 * rows, chans)
    low = jnp.dot(z, low_ref[...], preferred_element_type=f32)
    high = jnp.dot(z, high_ref[...], preferred_element_type=f32)
    other = tiles - 1 - step
    for tile, own, far in ((step, low, high), (other, high, low)):
        cols = pl.ds(pl.multiple_of(lax.rem(tile, per) * size, size), size)
        out_ref[tile // per, :, cols] = (own[:rows] + turned(far[rows:])).astype(bf16)


def output(z, out_weight, parts):
    _, rows, chans = z.shape
    width = out_weight.shape[1]
    each = width // parts
    size = min(512, each)
    tiles = width // size
    return pl.pallas_call(
        output_kernel,
        grid=(tiles // 2,),
        in_specs=[
            pl.BlockSpec((2, rows, chans), lambda i: (0, 0, 0)),
            pl.BlockSpec((chans, size), lambda i: (0, i)),
            pl.BlockSpec((chans, size), lambda i: (0, tiles - 1 - i)),
        ],
        out_specs=pl.BlockSpec((parts, rows, each), lambda i: (0, 0, 0)),
        out_shape=jax.ShapeDtypeStruct((parts, rows, each), bf16),
        compiler_params=pltpu.CompilerParams(vmem_limit_bytes=LIMIT),
        name="output",
    )(z, out_weight, out_weight)


def body(
    hidden, norm_gain, value_weight, gate_weight, value_taps, gate_taps, rates, residues, out_weight
):
    parts = 1
    rows = hidden.shape[0] // parts
    wholes = [
        gather(hidden[part * rows : (part + 1) * rows], "tp", line_kernel, part) for part in range(parts)
    ]
    proj = ()
    for part, whole in enumerate(wholes):
        proj = project(whole, part, parts, norm_gain, value_weight, gate_weight, proj)
    sent, fore, back = local_states(*proj, value_taps, rates)
    everyone = gather(sent, "seq", direct_kernel, parts)
    place = lax.axis_index("seq").astype(jnp.int32).reshape(1)
    z = gated(place, *proj, value_taps, gate_taps, rates, residues, fore, back, everyone)
    term = output(z, out_weight, lax.axis_size("tp"))
    return scatter_sum(term, "tp", parts + 1)


def solution(mesh):
    in_specs = (
        P("seq", "tp"),
        P(),
        P(None, "tp"),
        P(None, "tp"),
        P(None, "tp"),
        P(None, "tp"),
        P(None, "tp"),
        P(None, "tp"),
        P("tp", None),
    )
    out_specs = P("seq", "tp")
    return jax.shard_map(body, mesh=mesh, in_specs=in_specs, out_specs=out_specs, check_vma=False)
```
